512 devices in a mesh: row: 16 (over x, z_lo), col: 32 (over y, z_hi, core).
Axes of the slice: x: 4, y: 8, z: 8 (z_hi: 2, z_lo: 4; z = z_hi * 4 + z_lo), core: 2. Of those that a mesh axis runs over, the one named last changes fastest.
Arguments:
- out_grads: bfloat16 [896, 8192], P('row', 'col'), may hold values from -6 to 6
- inputs: bfloat16 [896, 8192], P('col', 'row'), may hold values from -6 to 6
- basis_out: bfloat16 [8192, 8192], P('col', 'row'), may hold values from -0.0625 to 0.0625
- basis_in: bfloat16 [8192, 8192], P('row', 'col'), may hold values from -0.0625 to 0.0625
- eig_out: float32 [8192], P('row'), may hold values from 0.05 to 5
- eig_in: float32 [8192], P('col'), may hold values from 0.05 to 5
- pair_order: int32 [896], replicated, may hold values from 0 to 895, each once
- length_bucket: int32 [896], replicated, may hold values from 0 to 7
Outputs:
- ihvp: float32 [128, 8192], P('col', 'row')
The draws below stay inside these ranges and needn't reach their ends.
All inputs are finite; a program needn't handle non-finite values.
Results may differ from the reference program's by a relative error of at most 0.0044.
Values may be sent and summed in bfloat16 or wider, within the bound.
No kernel may reach another device: no remote copies, remote signals or barrier semaphores. Data moves between devices by JAX's collectives and lax.ppermute only.
A program may use at most 64 MiB of HBM per device.

```python
import math
import jax
import jax.numpy as jnp
from jax import lax

D = 8192
TOK = 896
OUT = 128
OUT_BLK = 4
N_COL = 32


def plant(drawn, rng, least, largest):
    shape = drawn.shape
    spot = [jax.random.randint(jax.random.fold_in(rng, axis), (), 0, shape[axis]) for axis in range(len(shape))]
    drawn = drawn.at[tuple(spot)].set(least)
    longest = shape.index(max(shape))
    spot[longest] = (spot[longest] + 1) % shape[longest]
    return drawn.at[tuple(spot)].set(largest)


def steps_of(own_key, shape, split, least, top_value):
    gain, own = 1.0, jax.random.fold_in(own_key, 6)
    for position, shards_of in split:
        steps = jnp.exp(jax.random.uniform(jax.random.fold_in(own, position), (shards_of,), jnp.float32, least / len(split), top_value / len(split)))
        gain = gain * jnp.repeat(steps, shape[position] // shards_of).reshape([-1 if axis == position else 1 for axis in range(len(shape))])
    return gain


def centred(key, shape, width, reach, split=(), kind=jnp.bfloat16):
    result = jax.random.normal(key, shape, jnp.float32) * width
    if len(split) > 0:
        result = steps_of(key, shape, split, -0.22, 0.18) * result
    return jnp.clip(result, min=-reach, max=reach).astype(kind)


def setup_inputs(seed: int = 0) -> dict:
    streams_of = jax.random.split(jax.random.key(seed), 9)
    return {
        "out_grads": centred(streams_of[0], (TOK, D), 1.0, 6.0, ((0, 16), (1, 32))),
        "inputs": centred(streams_of[1], (TOK, D), 1.0, 6.0, ((0, 32), (1, 16))),
        "basis_out": centred(streams_of[2], (D, D), D ** -0.5, 0.0625, ((0, 32), (1, 16))),
        "basis_in": centred(streams_of[3], (D, D), D ** -0.5, 0.0625, ((0, 16), (1, 32))),
        "eig_out": jnp.clip(jnp.exp(math.log(5.0) - 4.6051702 * jax.random.uniform(streams_of[4], (D,), jnp.float32) ** steps_of(streams_of[4], (D,), ((0, 16),), -0.2, 0.2)), 0.05, 5.0),
        "eig_in": jnp.clip(jnp.exp(math.log(5.0) - 4.6051702 * jax.random.uniform(streams_of[5], (D,), jnp.float32) ** steps_of(streams_of[5], (D,), ((0, 32),), -0.2, 0.2)), 0.05, 5.0),
        "pair_order": jax.random.permutation(streams_of[6], TOK).astype(jnp.int32),
        "length_bucket": plant(jax.random.randint(streams_of[7], (TOK,), 0, 8), jax.random.fold_in(streams_of[7], 1), 0, 7).astype(jnp.int32),
    }


DAMPING = 0.1

def reference(out_grads, inputs, basis_out, basis_in, eig_out, eig_in, pair_order, length_bucket):
    positions = jnp.zeros((TOK,), jnp.int32).at[pair_order].set(jnp.arange(TOK, dtype=jnp.int32))
    pair_signs = jnp.where(positions % 2 == 0, 1.0, -1.0).astype(jnp.float32)
    weights = pair_signs / jnp.sqrt((1.0 + length_bucket.astype(jnp.float32)) * TOK)
    rot_out = (jnp.dot(out_grads, basis_out, preferred_element_type=jnp.float32) * weights[:, None]).astype(jnp.bfloat16)
    rot_in = jnp.dot(inputs, basis_in, preferred_element_type=jnp.float32).astype(jnp.bfloat16)
    middle = lax.dot_general(rot_out, rot_in, (((0,), (0,)), ((), ())), preferred_element_type=jnp.float32)
    scaled = (middle / (eig_out[:, None] * eig_in[None, :] + DAMPING)).astype(jnp.bfloat16)
    slab = basis_out.reshape(N_COL, D // N_COL, D)[:, :OUT_BLK, :].reshape(OUT, D)
    left = jnp.dot(slab, scaled, preferred_element_type=jnp.float32).astype(jnp.bfloat16)
    return lax.dot_general(left, basis_in, (((1,), (1,)), ((), ())), preferred_element_type=jnp.float32)
```

```python
import jax
import jax.numpy as jnp
from jax import lax
from jax.sharding import Mesh, PartitionSpec as P

DAMPING = 0.1
PAD = 32
ROW = ("x", "zl")
COL = ("y", "zh")
BF = jnp.bfloat16
F32 = jnp.float32


def dot(a, b, contract):
    return lax.dot_general(a, b, (contract, ((), ())), preferred_element_type=F32)


def gather(block, axes):
    size = lax.axis_size(axes)
    copies = jnp.broadcast_to(block[None], (size, *block.shape))
    return lax.all_to_all(copies, axes, 0, 0, tiled=True)


def scatter_sum(terms, axes):
    size = lax.axis_size(axes)
    parts = terms.astype(BF).reshape(size, -1, terms.shape[-1])
    return jnp.sum(lax.all_to_all(parts, axes, 0, 0, tiled=True).astype(F32), axis=0)


def shards(out_grads, inputs, basis_out, basis_in, eig_out, eig_in, pair_order, length_bucket):
    tokens = pair_order.shape[0]
    share = inputs.shape[0]
    blocks = tokens // (2 * share)
    slab_rows = PAD - share
    core = lax.axis_index("core")
    zh = lax.axis_index("zh")

    row = lax.broadcasted_iota(jnp.int32, (blocks, PAD), 1)
    token = (2 * lax.broadcasted_iota(jnp.int32, (blocks, PAD), 0) + core) * share + row
    token = jnp.where(row < share, token, -1).reshape(1, blocks * PAD)
    hit = pair_order[:, None] == token
    place = lax.broadcasted_iota(jnp.int32, (tokens, 1), 0)
    sign = jnp.sum(jnp.where(hit, jnp.where(place % 2 == 0, 1.0, -1.0), 0.0), axis=0)
    own_bucket = jnp.sum(
        jnp.where(lax.broadcasted_iota(jnp.int32, (tokens, 1), 0) == token, length_bucket[:, None], 0), axis=0
    )
    weights = sign / jnp.sqrt((1.0 + own_bucket.astype(F32)) * tokens)

    in_rows = jnp.concatenate([inputs, basis_out[:slab_rows]], axis=0)
    in_far = lax.ppermute(in_rows, "zh", [(0, 1), (1, 0)])
    grads = lax.all_to_all(out_grads, "core", 0, 1, tiled=True)
    grads = jnp.pad(grads, ((0, slab_rows), (0, 0)))
    basis_out2 = lax.all_gather(basis_out, "core", axis=0, tiled=True)
    basis_in2 = lax.all_gather(basis_in, "core", axis=0)
    eig_in2 = lax.all_gather(eig_in, "core", axis=0, tiled=True)

    grads_all = gather(grads, ROW).reshape(-1, grads.shape[1])
    part_out = dot(basis_out2, grads_all, ((0,), (1,)))

    in_pair = jnp.stack([jnp.where(zh == 0, in_rows, in_far), jnp.where(zh == 0, in_far, in_rows)])
    in_all = gather(in_pair, "y").reshape(blocks, PAD, -1)
    slab = in_all[:, share:].reshape(blocks * slab_rows, -1)
    in_all = in_all.reshape(blocks * PAD, -1)
    part_in = jnp.concatenate([dot(basis_in2[k], in_all, ((0,), (1,))) for k in range(2)])

    sum_out = scatter_sum(part_out, "y")
    sum_out = sum_out + lax.ppermute(sum_out, "zh", [(0, 1), (1, 0)])
    rot_in = scatter_sum(part_in, ROW).astype(BF)
    rot_out = (sum_out * weights).astype(BF)
    rot_out = gather(rot_out, "y").reshape(-1, blocks * PAD)
    rot_in = gather(rot_in, ROW).reshape(-1, blocks * PAD)
    rot_out = lax.all_gather(rot_out, "core", axis=0)
    rot_in = lax.all_gather(rot_in, "core", axis=0)
    middle = sum(dot(rot_out[k], rot_in[k], ((1,), (1,))) for k in range(2))
    scaled = (middle / (eig_out[:, None] * eig_in2[None, :] + DAMPING)).astype(BF)

    left = dot(slab, scaled, ((1,), (0,)))
    for axis in ROW:
        left = jnp.sum(gather(left.astype(BF), axis).astype(F32), axis=0)
    left = left.astype(BF)
    half = basis_in.shape[1]
    final = sum(
        dot(left[:, k * half : (k + 1) * half], basis_in2[k], ((1,), (1,))) for k in range(2)
    )
    return scatter_sum(final, COL)


def solution(mesh):
    fine = Mesh(mesh.devices.reshape(4, 4, 8, 2, 2), ("x", "zl", "y", "zh", "core"))
    row, col = ROW, (*COL, "core")
    return jax.shard_map(
        shards,
        mesh=fine,
        in_specs=(P(row, col), P(col, row), P(col, row), P(row, col), P(row), P(col), P(), P()),
        out_specs=P(col, row),
        check_vma=False,
    )
```

```python
import jax
import jax.numpy as jnp
import numpy as np
from jax import lax
from jax.sharding import Mesh, PartitionSpec as P

DAMPING = 0.1
PAD = 32
AXES = ("x", "zl", "y", "zh", "core")
SIZES = (4, 4, 8, 2, 2)
BF = jnp.bfloat16
F32 = jnp.float32
SWAP = [(0, 1), (1, 0)]

INDEX = np.arange(512).reshape(16, 16, 2)
ROWS = [INDEX[:, q, :].T.tolist() for q in range(16)]
COLS = [INDEX[r, :, :].T.tolist() for r in range(16)]
ROW_COL = [g[0] for g in ROWS] + [g[1] for g in COLS]
COL_ROW = [g[0] for g in COLS] + [g[1] for g in ROWS]


def dot(a, b, contract):
    return lax.dot_general(a, b, (contract, ((), ())), preferred_element_type=F32)


def exchange(parts, groups):
    return lax.all_to_all(parts, AXES, 0, 0, axis_index_groups=groups, tiled=True)


def copies(block, n):
    return jnp.broadcast_to(block[None], (n, *block.shape))


def shards(out_grads, inputs, basis_out, basis_in, eig_out, eig_in, pair_order, length_bucket):
    tokens, share = pair_order.shape[0], inputs.shape[0]
    n, extra, half = 16, PAD - share, basis_in.shape[1]
    first = lax.axis_index("core") == 0

    row = lax.broadcasted_iota(jnp.int32, (2 * n, PAD), 1)
    token = lax.broadcasted_iota(jnp.int32, (2 * n, PAD), 0) * share + row
    token = jnp.where(row < share, token, -1).reshape(1, 2 * n * PAD)
    place = lax.broadcasted_iota(jnp.int32, (tokens, 1), 0)
    parity = jnp.where(place % 2 == 0, 1.0, -1.0)
    sign = jnp.sum(jnp.where(pair_order[:, None] == token, parity, 0.0), axis=0)
    bucket = jnp.sum(jnp.where(place == token, length_bucket[:, None], 0), axis=0)
    weights = sign / jnp.sqrt((1.0 + bucket.astype(F32)) * tokens)
    weights = jnp.where(first, weights, 1.0)

    in_rows = jnp.concatenate([inputs, basis_out[:extra]], axis=0)
    grads = jnp.pad(out_grads.reshape(2, share, half), ((0, 0), (0, extra), (0, 0)))
    grads = jnp.concatenate([grads[0], grads[1]], axis=1)
    far = lax.ppermute(jnp.where(first, in_rows, grads), "core", SWAP)
    blocks = jnp.stack(
        [
            jnp.where(
                first,
                jnp.concatenate([s[:, k * half : (k + 1) * half] for s in (grads, far)], axis=1),
                (far, in_rows)[k],
            )
            for k in range(2)
        ]
    )
    rows = exchange(copies(blocks.reshape(2 * PAD, -1), n), ROW_COL)
    rows = rows.reshape(2 * n * PAD, -1)

    out_far = lax.ppermute(basis_out, "core", SWAP)
    in_far = lax.ppermute(basis_in, "core", SWAP)
    eig_far = lax.ppermute(eig_in, "core", SWAP)
    basis_in2 = jnp.where(
        first, jnp.concatenate([basis_in, in_far], axis=1), jnp.concatenate([in_far, basis_in], axis=1)
    )
    eig_in2 = jnp.where(first, jnp.concatenate([eig_in, eig_far]), jnp.concatenate([eig_far, eig_in]))
    basis = jnp.where(first, jnp.concatenate([basis_out, out_far], axis=0), basis_in2)

    part = dot(basis, rows, ((0,), (1,))).astype(BF)
    part = exchange(part.reshape(n, -1, part.shape[1]), COL_ROW)
    rot = (jnp.sum(part.astype(F32), axis=0) * weights).astype(BF)
    rot = exchange(copies(rot, n), COL_ROW).reshape(-1, rot.shape[1])

    slabs = rows.reshape(n, 2, PAD, -1)[:, :, share:]
    slabs = [slabs[:, k].reshape(n * extra, -1) for k in range(2)]
    slab = jnp.where(first, lax.ppermute(slabs[0], "core", SWAP), slabs[1])

    middle = dot(rot, lax.ppermute(rot, "core", SWAP), ((1,), (1,)))
    down, across = jnp.where(first, eig_out, eig_in2), jnp.where(first, eig_in2, eig_out)
    scaled = (middle / (down[:, None] * across[None, :] + DAMPING)).astype(BF)
    left = jnp.where(first, dot(slab, scaled, ((1,), (0,))), dot(slab, scaled, ((1,), (1,))))

    left = jnp.sum(lax.all_to_all(copies(left.astype(BF), 4), "x", 0, 0, tiled=True).astype(F32), axis=0)
    left = jnp.sum(lax.all_to_all(copies(left, 4), "zl", 0, 0, tiled=True), axis=0).astype(BF)
    final = dot(left, basis_in2, ((1,), (1,)))
    final = lax.all_to_all(final.reshape(n, -1, final.shape[1]), ("y", "zh"), 0, 0, tiled=True)
    return jnp.sum(final, axis=0)


def solution(mesh):
    fine = Mesh(mesh.devices.reshape(SIZES), AXES)
    row, col = AXES[:2], AXES[2:]
    return jax.shard_map(
        shards,
        mesh=fine,
        in_specs=(P(row, col), P(col, row), P(col, row), P(row, col), P(row), P(col), P(), P()),
        out_specs=P(col, row),
        check_vma=False,
    )
```

```python
import jax
import jax.numpy as jnp
import numpy as np
from jax import lax
from jax.sharding import Mesh, PartitionSpec as P

DAMPING = 0.1
AXES = ("x", "zl", "y", "zh", "core")
SIZES = (4, 4, 8, 2, 2)
BF = jnp.bfloat16
F32 = jnp.float32
SWAP = [(0, 1), (1, 0)]

INDEX = np.arange(512).reshape(4, 2, 2, 8, 2, 2)


def lists(order, size):
    return INDEX.transpose(order).reshape(2, -1, size).tolist()


NEAR_PAIR, NEAR_EIGHT = lists((5, 0, 1, 3, 4, 2), 2), lists((5, 2, 3, 4, 0, 1), 8)
SKIP_PAIR, SKIP_EIGHT = lists((5, 0, 2, 3, 4, 1), 2), lists((5, 1, 3, 4, 0, 2), 8)
COL_PAIR, COL_EIGHT = lists((5, 0, 1, 2, 3, 4), 2), lists((5, 0, 1, 2, 4, 3), 8)
PAIR_IN = [(g[i], g[1 - i]) for g in NEAR_PAIR[0] + COL_PAIR[1] for i in range(2)]
PAIR_MID = [(g[i], g[1 - i]) for g in COL_PAIR[0] + SKIP_PAIR[1] for i in range(2)]
EIGHT_IN = NEAR_EIGHT[0] + COL_EIGHT[1]
EIGHT_MID = COL_EIGHT[0] + SKIP_EIGHT[1]


def dot(a, b, contract):
    return lax.dot_general(a, b, (contract, ((), ())), preferred_element_type=F32)


def exchange(parts, groups):
    return lax.all_to_all(parts, AXES, 0, 0, axis_index_groups=groups, tiled=True)


def copies(block, n):
    return jnp.broadcast_to(block[None], (n, *block.shape))


def three(value):
    out = []
    for _ in range(3):
        out.append(lax.reduce_precision(value, 8, 7))
        value = value - out[-1]
    return [v.astype(BF) for v in out]


def shards(out_grads, inputs, basis_out, basis_in, eig_out, eig_in, pair_order, length_bucket):
    tokens, share, block = pair_order.shape[0], inputs.shape[0], out_grads.shape[0]
    half = basis_in.shape[1]
    extra = 32 - share
    n = 16
    first = lax.axis_index("core") == 0
    zh, zl = lax.axis_index("zh"), lax.axis_index("zl")

    slab_own = basis_out[:extra]
    eig3 = jnp.concatenate([*three(eig_in), jnp.zeros((half,), BF)]).reshape(2, 2 * half)
    eig3 = jnp.pad(eig3, ((0, 6), (0, 0)))
    grads = jnp.pad(out_grads, ((0, 64 - block), (0, 0)))
    send = jnp.where(
        first,
        jnp.concatenate([inputs, slab_own, eig3], axis=0),
        jnp.concatenate([jnp.concatenate([grads[:32], grads[32:]], axis=1), eig3], axis=0),
    )
    far = lax.ppermute(send, "core", SWAP)
    far_grads = jnp.concatenate([far[:32, :half], far[:32, half:]], axis=0)
    rows = jnp.where(
        first,
        jnp.concatenate([grads, far_grads], axis=1),
        jnp.concatenate([far[:share], inputs, far[share:32], slab_own], axis=0),
    )
    eig_far = far[32:34].reshape(4, half).astype(F32)
    eig_far = eig_far[0] + eig_far[1] + eig_far[2]
    eig_in2 = jnp.where(first, jnp.concatenate([eig_in, eig_far]), jnp.concatenate([eig_far, eig_in]))

    rows_far = lax.ppermute(rows, AXES, PAIR_IN)
    out_far = lax.ppermute(basis_out, "core", SWAP)
    in_far = lax.ppermute(basis_in, "core", SWAP)
    basis_in2 = jnp.where(
        first, jnp.concatenate([basis_in, in_far], axis=1), jnp.concatenate([in_far, basis_in], axis=1)
    )
    basis = jnp.where(first, jnp.concatenate([basis_out, out_far], axis=0), basis_in2)
    low = jnp.where(first, zl % 2, zh) == 0
    rows = jnp.stack([jnp.where(low, rows, rows_far), jnp.where(low, rows_far, rows)])

    place = lax.broadcasted_iota(jnp.int32, (tokens, 1), 0)
    token = lax.broadcasted_iota(jnp.int32, (1, tokens), 1)
    parity = jnp.where(place % 2 == 0, 1.0, -1.0)
    sign = jnp.sum(jnp.where(pair_order[:, None] == token, parity, 0.0), axis=0)
    weights = sign / jnp.sqrt((1.0 + length_bucket.astype(F32)) * tokens)
    weights = jnp.where(first, weights, 1.0)

    rows, basis, basis_in2, weights, eig_in2 = lax.optimization_barrier(
        (rows, basis, basis_in2, weights, eig_in2)
    )
    rows = exchange(copies(rows, 8), EIGHT_IN).reshape(n, 64, -1)

    slab0 = rows[:, block : block + extra].reshape(n * extra, -1)
    slab1 = rows[:, block + extra :].reshape(n * extra, -1)
    part = dot(basis, rows[:, :block].reshape(tokens, -1), ((0,), (1,))).astype(BF)
    part = exchange(part.reshape(8, -1, tokens), EIGHT_MID)
    total = jnp.sum(part.astype(F32), axis=0)
    total_far = lax.ppermute(total.astype(BF), AXES, PAIR_MID)
    slab = jnp.where(first, lax.ppermute(slab0, "core", SWAP), slab1)
    rot = ((total + total_far.astype(F32)) * weights).astype(BF)
    rot, slab = lax.optimization_barrier((rot, slab))
    rot = exchange(copies(rot, 8), EIGHT_MID).reshape(-1, tokens)

    middle = dot(rot, lax.ppermute(rot, "core", SWAP), ((1,), (1,)))
    down, across = jnp.where(first, eig_out, eig_in2), jnp.where(first, eig_in2, eig_out)
    scaled = (middle / (down[:, None] * across[None, :] + DAMPING)).astype(BF)
    left = jnp.where(first, dot(slab, scaled, ((1,), (0,))), dot(slab, scaled, ((1,), (1,))))

    left = lax.all_to_all(left.reshape(n, -1, left.shape[1]), ("x", "zl"), 0, 0, tiled=True)
    left = jnp.sum(left, axis=0).astype(BF)
    left = lax.all_to_all(copies(left, n), ("x", "zl"), 0, 0, tiled=True)
    left = left.reshape(-1, left.shape[2])
    final = dot(left, basis_in2, ((1,), (1,)))
    final = lax.all_to_all(final.reshape(n, -1, final.shape[1]), ("y", "zh"), 0, 0, tiled=True)
    return jnp.sum(final, axis=0)


def solution(mesh):
    fine = Mesh(mesh.devices.reshape(SIZES), AXES)
    row, col = AXES[:2], AXES[2:]
    return jax.shard_map(
        shards,
        mesh=fine,
        in_specs=(P(row, col), P(col, row), P(col, row), P(row, col), P(row), P(col), P(), P()),
        out_specs=P(col, row),
        check_vma=False,
    )
```

```python
import jax
import jax.numpy as jnp
import numpy as np
from jax import lax
from jax.sharding import Mesh, PartitionSpec as P

DAMPING = 0.1
AXES = ("x", "zl", "y", "zh", "core")
SIZES = (4, 4, 8, 2, 2)
BF = jnp.bfloat16
F32 = jnp.float32
SWAP = [(0, 1), (1, 0)]

INDEX = np.arange(512).reshape(4, 2, 2, 8, 2, 2)


def lists(order, size):
    return INDEX.transpose(order).reshape(2, -1, size).tolist()


ROW_PAIR, ROW_EIGHT = lists((5, 0, 2, 3, 4, 1), 2), lists((5, 1, 3, 4, 0, 2), 8)
COL_PAIR, COL_EIGHT = lists((5, 0, 1, 2, 3, 4), 2), lists((5, 0, 1, 2, 4, 3), 8)
COL_ALL = lists((5, 0, 1, 2, 4, 3), 16)
EIGHT_IN = ROW_EIGHT[0] + COL_EIGHT[1]
EIGHT_MID = COL_EIGHT[0] + ROW_EIGHT[1]
PAIR_IN = [(g[i], g[1 - i]) for g in ROW_PAIR[0] + COL_PAIR[1] for i in range(2)]
PAIR_MID = [(g[i], g[1 - i]) for g in COL_PAIR[0] + ROW_PAIR[1] for i in range(2)]
CROSS = [(g[i], g[1 - i] + 1) for g in COL_PAIR[0] for i in range(2)]
CROSS += [(g[i], g[1 - i] - 1) for g in ROW_PAIR[1] for i in range(2)]


def dot(a, b, contract):
    return lax.dot_general(a, b, (contract, ((), ())), preferred_element_type=F32)


def exchange(parts, groups):
    return lax.all_to_all(parts, AXES, 0, 0, axis_index_groups=groups, tiled=True)


def copies(block, n):
    return jnp.broadcast_to(block[None], (n, *block.shape))


def shards(out_grads, inputs, basis_out, basis_in, eig_out, eig_in, pair_order, length_bucket):
    tokens, share, block = pair_order.shape[0], inputs.shape[0], out_grads.shape[0]
    half = basis_in.shape[1]
    extra = 32 - share
    n = 16
    first = lax.axis_index("core") == 0
    zh, zl = lax.axis_index("zh"), lax.axis_index("zl")

    acts = jnp.concatenate([inputs, basis_out[:extra]], axis=0)
    grads = jnp.pad(out_grads, ((0, 64 - block), (0, 0)))
    grads = jnp.concatenate([grads[:32], grads[32:]], axis=1)
    kept, given = jnp.where(first, grads, acts), jnp.where(first, acts, grads)
    kept_far = lax.ppermute(kept, AXES, PAIR_IN)
    cross_far = lax.ppermute(given, AXES, CROSS)
    given_far = lax.ppermute(given, "core", SWAP)

    def joined(mine, other):
        lanes = [[p[:, :half], p[:, half:]] for p in (mine, other)]
        as_grads = jnp.concatenate([jnp.concatenate(p, axis=0) for p in lanes], axis=1)
        as_acts = jnp.concatenate([other[:share], mine[:share], other[share:], mine[share:]], axis=0)
        return jnp.where(first, as_grads, as_acts)

    rows, rows_far = joined(kept, given_far), joined(kept_far, cross_far)
    low = jnp.where(first, zl // 2, zh) == 0
    rows = jnp.stack([jnp.where(low, rows, rows_far), jnp.where(low, rows_far, rows)])

    late = lax.optimization_barrier((given_far, basis_out, basis_in, eig_in, pair_order, length_bucket))
    basis_out_late, basis_in_late, eig_late, pair_order, length_bucket = late[1:]
    out_far = lax.ppermute(basis_out_late, "core", SWAP)
    in_far = lax.ppermute(basis_in_late, "core", SWAP)
    basis_in2 = jnp.where(
        first, jnp.concatenate([basis_in, in_far], axis=1), jnp.concatenate([in_far, basis_in], axis=1)
    )
    basis = jnp.where(first, jnp.concatenate([basis_out, out_far], axis=0), basis_in2)
    eig_far = lax.ppermute(eig_late, "core", SWAP)
    eig_in2 = jnp.where(first, jnp.concatenate([eig_in, eig_far]), jnp.concatenate([eig_far, eig_in]))
    place = lax.broadcasted_iota(jnp.int32, (tokens, 1), 0)
    token = lax.broadcasted_iota(jnp.int32, (1, tokens), 1)
    parity = jnp.where(place % 2 == 0, 1.0, -1.0)
    sign = jnp.sum(jnp.where(pair_order[:, None] == token, parity, 0.0), axis=0)
    weights = sign / jnp.sqrt((1.0 + length_bucket.astype(F32)) * tokens)
    weights = jnp.where(first, weights, 1.0)

    rows, basis, basis_in2, eig_in2, weights = lax.optimization_barrier(
        (rows, basis, basis_in2, eig_in2, weights)
    )
    rows = exchange(copies(rows, 8), EIGHT_IN)
    ordered = rows[:, :, :block].reshape(tokens, -1)
    paired = rows.reshape(4, 2, 2, 64, -1).swapaxes(1, 2)[:, :, :, :block].reshape(tokens, -1)
    part = dot(basis, jnp.where(first, paired, ordered), ((0,), (1,))).astype(BF)
    part = exchange(part.reshape(8, -1, tokens), EIGHT_MID)
    part, rows = lax.optimization_barrier((part, rows))
    total = jnp.sum(part.astype(F32), axis=0)
    total_far = lax.ppermute(total.astype(BF), AXES, PAIR_MID)
    slab0, slab1 = (
        rows[:, :, block + k * extra : block + (k + 1) * extra].swapaxes(0, 1).reshape(n * extra, -1)
        for k in range(2)
    )
    rot = ((total + total_far.astype(F32)) * weights).astype(BF)
    rot, slab0, slab1 = lax.optimization_barrier((rot, slab0, slab1))
    rot = exchange(copies(rot, 8), EIGHT_MID).reshape(-1, tokens)
    rot, slab0 = lax.optimization_barrier((rot, slab0))
    rot_far = lax.ppermute(rot, "core", SWAP)
    slab = jnp.where(first, lax.ppermute(slab0, "core", SWAP), slab1)

    middle = dot(rot, rot_far, ((1,), (1,)))
    down, across = jnp.where(first, eig_out, eig_in2), jnp.where(first, eig_in2, eig_out)
    scaled = (middle / (down[:, None] * across[None, :] + DAMPING)).astype(BF)
    left = jnp.where(first, dot(slab, scaled, ((1,), (0,))), dot(slab, scaled, ((1,), (1,))))

    left = lax.all_to_all(left.reshape(n, -1, left.shape[1]), ("x", "zl"), 0, 0, tiled=True)
    left = jnp.sum(left, axis=0).astype(BF)
    left = lax.all_to_all(copies(left, n), ("x", "zl"), 0, 0, tiled=True)
    left = left.reshape(-1, left.shape[2])
    final = dot(left, basis_in2, ((1,), (1,)))
    final = exchange(final.reshape(n, -1, final.shape[1]), COL_ALL[0] + COL_ALL[1])
    return jnp.sum(final, axis=0)


def solution(mesh):
    fine = Mesh(mesh.devices.reshape(SIZES), AXES)
    row, col = AXES[:2], AXES[2:]
    return jax.shard_map(
        shards,
        mesh=fine,
        in_specs=(P(row, col), P(col, row), P(col, row), P(row, col), P(row), P(col), P(), P()),
        out_specs=P(col, row),
        check_vma=False,
    )
```

```python
import jax
import jax.numpy as jnp
import numpy as np
from jax import lax
from jax.sharding import Mesh, PartitionSpec as P

DAMPING = 0.1
AXES = ("x", "zl", "y", "zh", "core")
SIZES = (4, 4, 8, 2, 2)
BF = jnp.bfloat16
F32 = jnp.float32
SWAP = [(0, 1), (1, 0)]

INDEX = np.arange(512).reshape(4, 2, 2, 8, 2, 2)


def lists(order, size):
    return INDEX.transpose(order).reshape(2, -1, size).tolist()


ROW_PAIR, ROW_EIGHT = lists((5, 0, 2, 3, 4, 1), 2), lists((5, 1, 3, 4, 0, 2), 8)
COL_PAIR, COL_EIGHT = lists((5, 0, 1, 2, 3, 4), 2), lists((5, 0, 1, 2, 4, 3), 8)
COL_ALL = lists((5, 0, 1, 2, 4, 3), 16)
EIGHT_IN = ROW_EIGHT[0] + COL_EIGHT[1]
EIGHT_MID = COL_EIGHT[0] + ROW_EIGHT[1]
PAIR_IN = [(g[i], g[1 - i]) for g in ROW_PAIR[0] + COL_PAIR[1] for i in range(2)]
PAIR_MID = [(g[i], g[1 - i]) for g in COL_PAIR[0] + ROW_PAIR[1] for i in range(2)]
CROSS = [(g[i], g[1 - i] + 1) for g in COL_PAIR[0] for i in range(2)]
CROSS += [(g[i], g[1 - i] - 1) for g in ROW_PAIR[1] for i in range(2)]


def dot(a, b, contract):
    return lax.dot_general(a, b, (contract, ((), ())), preferred_element_type=F32)


def exchange(parts, groups):
    return lax.all_to_all(parts, AXES, 0, 0, axis_index_groups=groups, tiled=True)


def copies(block, n):
    return jnp.broadcast_to(block[None], (n, *block.shape))


def three(value):
    out = []
    for _ in range(3):
        out.append(lax.reduce_precision(value, 8, 7))
        value = value - out[-1]
    return [v.astype(BF) for v in out]


def shards(out_grads, inputs, basis_out, basis_in, eig_out, eig_in, pair_order, length_bucket):
    tokens, share, block = pair_order.shape[0], inputs.shape[0], out_grads.shape[0]
    half = basis_in.shape[1]
    extra = 32 - share
    n = 16
    first = lax.axis_index("core") == 0
    zh, zl = lax.axis_index("zh"), lax.axis_index("zl")

    acts = jnp.concatenate([inputs, basis_out[:extra]], axis=0)
    grads = jnp.pad(out_grads, ((0, 64 - block), (0, 0)))
    grads = jnp.concatenate([grads[:32], grads[32:]], axis=1)
    kept, given = jnp.where(first, grads, acts), jnp.where(first, acts, grads)
    kept_far = lax.ppermute(kept, AXES, PAIR_IN)
    cross_far = lax.ppermute(given, AXES, CROSS)
    given_far = lax.ppermute(given, "core", SWAP)

    def joined(mine, other):
        lanes = [[p[:, :half], p[:, half:]] for p in (mine, other)]
        as_grads = jnp.concatenate([jnp.concatenate(p, axis=0) for p in lanes], axis=1)
        as_acts = jnp.concatenate([other[:share], mine[:share], other[share:], mine[share:]], axis=0)
        return jnp.where(first, as_grads, as_acts)

    rows, rows_far = joined(kept, given_far), joined(kept_far, cross_far)
    low = jnp.where(first, zl // 2, zh) == 0
    rows = jnp.stack([jnp.where(low, rows, rows_far), jnp.where(low, rows_far, rows)])

    late = lax.optimization_barrier((given_far, basis_out, basis_in, eig_in))
    out_far = lax.ppermute(late[1], "core", SWAP)
    packed = jnp.concatenate([late[2], jnp.stack(three(late[3])), jnp.zeros((13, half), BF)], axis=0)
    in_far, eig_far = jnp.split(lax.ppermute(packed, "core", SWAP), [basis_in.shape[0]])
    basis_in2 = jnp.where(
        first, jnp.concatenate([basis_in, in_far], axis=1), jnp.concatenate([in_far, basis_in], axis=1)
    )
    basis = jnp.where(first, jnp.concatenate([basis_out, out_far], axis=0), basis_in2)
    parity = jnp.where(jnp.arange(tokens) % 2 == 0, 1.0, -1.0)
    rows, basis, basis_in2, eig_far, parity = lax.optimization_barrier((rows, basis, basis_in2, eig_far, parity))
    rows = exchange(copies(rows, 8), EIGHT_IN)
    ordered = rows[:, :, :block].reshape(tokens, -1)
    paired = rows.reshape(4, 2, 2, 64, -1).swapaxes(1, 2)[:, :, :, :block].reshape(tokens, -1)
    part = dot(basis, jnp.where(first, paired, ordered), ((0,), (1,))).astype(BF)
    part = exchange(part.reshape(8, -1, tokens), EIGHT_MID)
    part, rows = lax.optimization_barrier((part, rows))
    total = jnp.sum(part.astype(F32), axis=0)
    total_far = lax.ppermute(total.astype(BF), AXES, PAIR_MID)
    slab0, slab1 = (
        rows[:, :, block + k * extra : block + (k + 1) * extra].swapaxes(0, 1).reshape(n * extra, -1)
        for k in range(2)
    )

    late = lax.optimization_barrier((part, pair_order, length_bucket, eig_far))
    _, pair_order, length_bucket, eig_far = late
    token = lax.broadcasted_iota(jnp.int32, (1, tokens), 1)
    sign = jnp.sum(jnp.where(pair_order[:, None] == token, parity[:, None], 0.0), axis=0)
    weights = sign / jnp.sqrt((1.0 + length_bucket.astype(F32)) * tokens)
    weights = jnp.where(first, weights, 1.0)
    eig_far = jnp.sum(eig_far.astype(F32), axis=0)
    eig_in2 = jnp.where(first, jnp.concatenate([eig_in, eig_far]), jnp.concatenate([eig_far, eig_in]))
    rot = ((total + total_far.astype(F32)) * weights).astype(BF)
    rot, slab0, slab1, eig_in2 = lax.optimization_barrier((rot, slab0, slab1, eig_in2))
    rot = exchange(copies(rot, 8), EIGHT_MID).reshape(-1, tokens)
    rot, slab0 = lax.optimization_barrier((rot, slab0))
    rot_far = lax.ppermute(rot, "core", SWAP)
    slab = jnp.where(first, lax.ppermute(slab0, "core", SWAP), slab1)

    middle = dot(rot, rot_far, ((1,), (1,)))
    down, across = jnp.where(first, eig_out, eig_in2), jnp.where(first, eig_in2, eig_out)
    scaled = (middle / (down[:, None] * across[None, :] + DAMPING)).astype(BF)
    left = jnp.where(first, dot(slab, scaled, ((1,), (0,))), dot(slab, scaled, ((1,), (1,))))

    left = lax.all_to_all(left.reshape(n, -1, left.shape[1]), ("x", "zl"), 0, 0, tiled=True)
    left = jnp.sum(left, axis=0).astype(BF)
    left = lax.all_to_all(copies(left, n), ("x", "zl"), 0, 0, tiled=True)
    left = left.reshape(-1, left.shape[2])
    final = dot(left, basis_in2, ((1,), (1,)))
    final = exchange(final.reshape(n, -1, final.shape[1]), COL_ALL[0] + COL_ALL[1])
    return jnp.sum(final, axis=0)


def solution(mesh):
    fine = Mesh(mesh.devices.reshape(SIZES), AXES)
    row, col = AXES[:2], AXES[2:]
    return jax.shard_map(
        shards,
        mesh=fine,
        in_specs=(P(row, col), P(col, row), P(col, row), P(row, col), P(row), P(col), P(), P()),
        out_specs=P(col, row),
        check_vma=False,
    )
```

```python
import jax
import jax.numpy as jnp
import numpy as np
from jax import lax
from jax.sharding import Mesh, PartitionSpec as P

DAMPING = 0.1
AXES = ("x", "zl", "y", "zh", "core")
SIZES = (4, 4, 8, 2, 2)
BF = jnp.bfloat16
F32 = jnp.float32
SWAP = [(0, 1), (1, 0)]

INDEX = np.arange(512).reshape(4, 2, 2, 8, 2, 2)


def lists(order, size):
    return INDEX.transpose(order).reshape(2, -1, size).tolist()


ROW_PAIR, ROW_EIGHT = lists((5, 0, 2, 3, 4, 1), 2), lists((5, 1, 3, 4, 0, 2), 8)
COL_PAIR, COL_EIGHT = lists((5, 0, 1, 2, 3, 4), 2), lists((5, 0, 1, 2, 4, 3), 8)
COL_ALL = lists((5, 0, 1, 2, 4, 3), 16)
EIGHT_IN = ROW_EIGHT[0] + COL_EIGHT[1]
EIGHT_MID = COL_EIGHT[0] + ROW_EIGHT[1]
PAIR_IN = [(g[i], g[1 - i]) for g in ROW_PAIR[0] + COL_PAIR[1] for i in range(2)]
PAIR_MID = [(g[i], g[1 - i]) for g in COL_PAIR[0] + ROW_PAIR[1] for i in range(2)]


def dot(a, b, contract):
    return lax.dot_general(a, b, (contract, ((), ())), preferred_element_type=F32)


def exchange(parts, groups):
    return lax.all_to_all(parts, AXES, 0, 0, axis_index_groups=groups, tiled=True)


def copies(block, n):
    return jnp.broadcast_to(block[None], (n, *block.shape))


def wide(tall_one):
    rows = tall_one.shape[0] // 2
    return jnp.concatenate([tall_one[:rows], tall_one[rows:]], axis=1)


def tall(wide_one):
    lanes = wide_one.shape[1] // 2
    return jnp.concatenate([wide_one[:, :lanes], wide_one[:, lanes:]], axis=0)


def three(value):
    out = []
    for _ in range(3):
        out.append(lax.reduce_precision(value, 8, 7))
        value = value - out[-1]
    return [v.astype(BF) for v in out]


def shards(out_grads, inputs, basis_out, basis_in, eig_out, eig_in, pair_order, length_bucket):
    tokens, share, block = pair_order.shape[0], inputs.shape[0], out_grads.shape[0]
    half = basis_in.shape[1]
    extra = 32 - share
    n = 16
    first = lax.axis_index("core") == 0
    zh, zl = lax.axis_index("zh"), lax.axis_index("zl")

    acts = jnp.concatenate([inputs, basis_out[:extra]], axis=0)
    grads = jnp.pad(out_grads, ((0, 64 - block), (0, 0)))
    grads = jnp.concatenate([grads[:32], grads[32:]], axis=1)
    kept = jnp.where(first, grads, acts)
    far = jnp.where(
        first, jnp.concatenate([acts, wide(basis_in)], axis=0), jnp.concatenate([grads, basis_out], axis=0)
    )
    far = lax.ppermute(far, "core", SWAP)
    far, basis_far = far[:32], far[32:]
    lanes = [[p[:, :half], p[:, half:]] for p in (kept, far)]
    as_grads = jnp.concatenate([jnp.concatenate(p, axis=0) for p in lanes], axis=1)
    as_acts = jnp.concatenate([far[:share], kept[:share], far[share:], kept[share:]], axis=0)
    rows = jnp.where(first, as_grads, as_acts)

    rows_far = lax.ppermute(rows, AXES, PAIR_IN)
    basis = jnp.where(
        first,
        jnp.concatenate([basis_out, basis_far], axis=0),
        jnp.concatenate([tall(basis_far), basis_in], axis=1),
    )
    low = jnp.where(first, zl // 2, zh) == 0
    rows = jnp.stack([jnp.where(low, rows, rows_far), jnp.where(low, rows_far, rows)])
    parity = jnp.where(jnp.arange(tokens) % 2 == 0, 1.0, -1.0)
    rows, basis, parity = lax.optimization_barrier((rows, basis, parity))
    rows = exchange(copies(rows, 8), EIGHT_IN)
    ordered = rows[:, :, :block].reshape(tokens, -1)
    paired = rows.reshape(4, 2, 2, 64, -1).swapaxes(1, 2)[:, :, :, :block].reshape(tokens, -1)
    part = dot(basis, jnp.where(first, paired, ordered), ((0,), (1,))).astype(BF)
    part = exchange(part.reshape(8, -1, tokens), EIGHT_MID)
    total = jnp.sum(part.astype(F32), axis=0)

    sent, *late = lax.optimization_barrier((total.astype(BF), pair_order, length_bucket))
    pair_order, length_bucket = late
    total_far = lax.ppermute(sent, AXES, PAIR_MID)
    token = lax.broadcasted_iota(jnp.int32, (1, tokens), 1)
    sign = jnp.sum(jnp.where(pair_order[:, None] == token, parity[:, None], 0.0), axis=0)
    weights = sign / jnp.sqrt((1.0 + length_bucket.astype(F32)) * tokens)
    weights = jnp.where(first, weights, 1.0)
    weights, rows, in_late, eig_late = lax.optimization_barrier((weights, rows, basis_in, eig_in))
    slab0, slab1 = (
        rows[:, :, block + k * extra : block + (k + 1) * extra].swapaxes(0, 1).reshape(n * extra, -1)
        for k in range(2)
    )
    eig3 = jnp.concatenate([*three(eig_late), jnp.zeros((half,), BF)]).reshape(2, 2 * half)
    packed = jnp.concatenate([slab0, wide(in_late), jnp.pad(eig3, ((0, 14), (0, 0)))], axis=0)
    rot = ((total + total_far.astype(F32)) * weights).astype(BF)
    rot, packed, slab1 = lax.optimization_barrier((rot, packed, slab1))
    rot = exchange(copies(rot, 8), EIGHT_MID).reshape(-1, tokens)
    rot, packed = lax.optimization_barrier((rot, packed))
    rot_far = lax.ppermute(rot, "core", SWAP)
    far = lax.ppermute(packed, "core", SWAP)
    slab = jnp.where(first, far[: slab1.shape[0]], slab1)
    eig_far = far[-16:-14].astype(F32).reshape(4, half)
    eig_far = eig_far[0] + eig_far[1] + eig_far[2]
    eig_in2 = jnp.where(first, jnp.concatenate([eig_in, eig_far]), jnp.concatenate([eig_far, eig_in]))
    in_far = tall(far[slab1.shape[0] : -16])
    basis_in2 = jnp.where(
        first, jnp.concatenate([basis_in, in_far], axis=1), jnp.concatenate([in_far, basis_in], axis=1)
    )

    middle = dot(rot, rot_far, ((1,), (1,)))
    down, across = jnp.where(first, eig_out, eig_in2), jnp.where(first, eig_in2, eig_out)
    scaled = (middle / (down[:, None] * across[None, :] + DAMPING)).astype(BF)
    left = jnp.where(first, dot(slab, scaled, ((1,), (0,))), dot(slab, scaled, ((1,), (1,))))

    left, basis_in2 = lax.optimization_barrier((left, basis_in2))
    left = lax.all_to_all(left.reshape(n, -1, left.shape[1]), ("x", "zl"), 0, 0, tiled=True)
    left = jnp.sum(left, axis=0).astype(BF)
    left = lax.all_to_all(copies(left, n), ("x", "zl"), 0, 0, tiled=True)
    left = left.reshape(-1, left.shape[2])
    final = dot(left, basis_in2, ((1,), (1,)))
    final = exchange(final.reshape(n, -1, final.shape[1]), COL_ALL[0] + COL_ALL[1])
    return jnp.sum(final, axis=0)


def solution(mesh):
    fine = Mesh(mesh.devices.reshape(SIZES), AXES)
    row, col = AXES[:2], AXES[2:]
    return jax.shard_map(
        shards,
        mesh=fine,
        in_specs=(P(row, col), P(col, row), P(col, row), P(row, col), P(row), P(col), P(), P()),
        out_specs=P(col, row),
        check_vma=False,
    )
```

```python
import jax
import jax.numpy as jnp
import numpy as np
from jax import lax
from jax.sharding import Mesh, PartitionSpec as P

DAMPING = 0.1
AXES = ("x", "zl", "y", "zh", "core")
SIZES = (4, 4, 8, 2, 2)
BF = jnp.bfloat16
F32 = jnp.float32
SWAP = [(0, 1), (1, 0)]

INDEX = np.arange(512).reshape(4, 2, 2, 8, 2, 2)


def lists(order, size):
    return INDEX.transpose(order).reshape(2, -1, size).tolist()


ROW_PAIR, ROW_EIGHT = lists((5, 0, 2, 3, 4, 1), 2), lists((5, 1, 3, 4, 0, 2), 8)
COL_PAIR, COL_EIGHT = lists((5, 0, 1, 2, 3, 4), 2), lists((5, 0, 1, 2, 4, 3), 8)
COL_ALL = lists((5, 0, 1, 2, 4, 3), 16)
EIGHT_IN = ROW_EIGHT[0] + COL_EIGHT[1]
EIGHT_MID = COL_EIGHT[0] + ROW_EIGHT[1]
PAIR_IN = [(g[i], g[1 - i]) for g in ROW_PAIR[0] + COL_PAIR[1] for i in range(2)]
PAIR_MID = [(g[i], g[1 - i]) for g in COL_PAIR[0] + ROW_PAIR[1] for i in range(2)]


def dot(a, b, contract):
    return lax.dot_general(a, b, (contract, ((), ())), preferred_element_type=F32)


def exchange(parts, groups):
    return lax.all_to_all(parts, AXES, 0, 0, axis_index_groups=groups, tiled=True)


def copies(block, n):
    return jnp.broadcast_to(block[None], (n, *block.shape))


def wide(tall_one):
    rows = tall_one.shape[0] // 2
    return jnp.concatenate([tall_one[:rows], tall_one[rows:]], axis=1)


def tall(wide_one):
    lanes = wide_one.shape[1] // 2
    return jnp.concatenate([wide_one[:, :lanes], wide_one[:, lanes:]], axis=0)


def three(value):
    out = []
    for _ in range(3):
        out.append(lax.reduce_precision(value, 8, 7))
        value = value - out[-1]
    return [v.astype(BF) for v in out]


def shards(out_grads, inputs, basis_out, basis_in, eig_out, eig_in, pair_order, length_bucket):
    tokens, share, block = pair_order.shape[0], inputs.shape[0], out_grads.shape[0]
    half = basis_in.shape[1]
    extra = 32 - share
    n = 16
    first = lax.axis_index("core") == 0
    zh, zl = lax.axis_index("zh"), lax.axis_index("zl")

    acts = jnp.concatenate([inputs, basis_out[:extra]], axis=0)
    grads = jnp.pad(out_grads, ((0, 64 - block), (0, 0)))
    grads = jnp.concatenate([grads[:32], grads[32:]], axis=1)
    kept = jnp.where(first, grads, acts)
    far = jnp.where(
        first, jnp.concatenate([acts, wide(basis_in)], axis=0), jnp.concatenate([grads, basis_out], axis=0)
    )
    far = lax.ppermute(far, "core", SWAP)
    far, basis_far = far[:32], far[32:]
    lanes = [[p[:, :half], p[:, half:]] for p in (kept, far)]
    as_grads = jnp.concatenate([jnp.concatenate(p, axis=0) for p in lanes], axis=1)
    as_acts = jnp.concatenate([far[:share], kept[:share], far[share:], kept[share:]], axis=0)
    rows = jnp.where(first, as_grads, as_acts)

    rows_far = lax.ppermute(rows, AXES, PAIR_IN)
    basis = jnp.where(
        first,
        jnp.concatenate([basis_out, basis_far], axis=0),
        jnp.concatenate([tall(basis_far), basis_in], axis=1),
    )
    late = lax.optimization_barrier((rows, basis_in, eig_in, pair_order, length_bucket))
    _, in_late, eig_late, pair_order, length_bucket = late
    parity = jnp.where(jnp.arange(tokens) % 2 == 0, 1.0, -1.0)
    token = lax.broadcasted_iota(jnp.int32, (1, tokens), 1)
    sign = jnp.sum(jnp.where(pair_order[:, None] == token, parity[:, None], 0.0), axis=0)
    weights = sign / jnp.sqrt((1.0 + length_bucket.astype(F32)) * tokens)
    weights = jnp.where(first, weights, 1.0)
    eig3 = jnp.concatenate([*three(eig_late), jnp.zeros((half,), BF)]).reshape(2, 2 * half)
    later = jnp.concatenate([wide(in_late), jnp.pad(eig3, ((0, 14), (0, 0)))], axis=0)
    low = jnp.where(first, zl // 2, zh) == 0
    rows = jnp.stack([jnp.where(low, rows, rows_far), jnp.where(low, rows_far, rows)])
    rows, basis, weights, later = lax.optimization_barrier((rows, basis, weights, later))
    rows = exchange(copies(rows, 8), EIGHT_IN)
    ordered = rows[:, :, :block].reshape(tokens, -1)
    paired = rows.reshape(4, 2, 2, 64, -1).swapaxes(1, 2)[:, :, :, :block].reshape(tokens, -1)
    part = dot(basis, jnp.where(first, paired, ordered), ((0,), (1,))).astype(BF)
    part = exchange(part.reshape(8, -1, tokens), EIGHT_MID)
    part, rows = lax.optimization_barrier((part, rows))
    total = jnp.sum(part.astype(F32), axis=0)

    total_far = lax.ppermute(total.astype(BF), AXES, PAIR_MID)
    slab0, slab1 = (
        rows[:, :, block + k * extra : block + (k + 1) * extra].swapaxes(0, 1).reshape(n * extra, -1)
        for k in range(2)
    )
    packed = jnp.concatenate([slab0, later], axis=0)
    rot = ((total + total_far.astype(F32)) * weights).astype(BF)
    rot, packed, slab1 = lax.optimization_barrier((rot, packed, slab1))
    rot = exchange(copies(rot, 8), EIGHT_MID).reshape(-1, tokens)
    rot, packed = lax.optimization_barrier((rot, packed))
    rot_far = lax.ppermute(rot, "core", SWAP)
    far = lax.ppermute(packed, "core", SWAP)
    rot_far, far = lax.optimization_barrier((rot_far, far))
    slab = jnp.where(first, far[: slab1.shape[0]], slab1)
    eig_far = far[-16:-14].astype(F32).reshape(4, half)
    eig_far = eig_far[0] + eig_far[1] + eig_far[2]
    eig_in2 = jnp.where(first, jnp.concatenate([eig_in, eig_far]), jnp.concatenate([eig_far, eig_in]))
    in_far = tall(far[slab1.shape[0] : -16])
    basis_in2 = jnp.where(
        first, jnp.concatenate([basis_in, in_far], axis=1), jnp.concatenate([in_far, basis_in], axis=1)
    )

    middle = dot(rot, rot_far, ((1,), (1,)))
    down, across = jnp.where(first, eig_out, eig_in2), jnp.where(first, eig_in2, eig_out)
    scaled = (middle / (down[:, None] * across[None, :] + DAMPING)).astype(BF)
    left = jnp.where(first, dot(slab, scaled, ((1,), (0,))), dot(slab, scaled, ((1,), (1,))))

    left, basis_in2 = lax.optimization_barrier((left, basis_in2))
    left = lax.all_to_all(left.reshape(n, -1, left.shape[1]), ("x", "zl"), 0, 0, tiled=True)
    left = jnp.sum(left, axis=0).astype(BF)
    left = lax.all_to_all(copies(left, n), ("x", "zl"), 0, 0, tiled=True)
    left = left.reshape(-1, left.shape[2])
    final = dot(left, basis_in2, ((1,), (1,)))
    final = exchange(final.reshape(n, -1, final.shape[1]), COL_ALL[0] + COL_ALL[1])
    return jnp.sum(final, axis=0)


def solution(mesh):
    fine = Mesh(mesh.devices.reshape(SIZES), AXES)
    row, col = AXES[:2], AXES[2:]
    return jax.shard_map(
        shards,
        mesh=fine,
        in_specs=(P(row, col), P(col, row), P(col, row), P(row, col), P(row), P(col), P(), P()),
        out_specs=P(col, row),
        check_vma=False,
    )
```

```python
import jax
import jax.numpy as jnp
import numpy as np
from jax import lax
from jax.sharding import Mesh, PartitionSpec as P

DAMPING = 0.1
AXES = ("x", "zl", "y", "zh", "core")
SIZES = (4, 4, 8, 2, 2)
BF = jnp.bfloat16
F32 = jnp.float32
SWAP = [(0, 1), (1, 0)]

INDEX = np.arange(512).reshape(4, 2, 2, 8, 2, 2)


def lists(order, size):
    return INDEX.transpose(order).reshape(2, -1, size).tolist()


ROW_PAIR, ROW_EIGHT = lists((5, 0, 2, 3, 4, 1), 2), lists((5, 1, 3, 4, 0, 2), 8)
COL_PAIR, COL_EIGHT = lists((5, 0, 1, 2, 3, 4), 2), lists((5, 0, 1, 2, 4, 3), 8)
COL_ALL = lists((5, 0, 1, 2, 4, 3), 16)
EIGHT_IN = ROW_EIGHT[0] + COL_EIGHT[1]
EIGHT_MID = COL_EIGHT[0] + ROW_EIGHT[1]
PAIR_IN = ROW_PAIR[0] + COL_PAIR[1]
PAIR_MID = COL_PAIR[0] + ROW_PAIR[1]


def dot(a, b, contract):
    return lax.dot_general(a, b, (contract, ((), ())), preferred_element_type=F32)


def exchange(parts, groups):
    return lax.all_to_all(parts, AXES, 0, 0, axis_index_groups=groups, tiled=True)


def both(block, groups):
    return lax.all_gather(block, AXES, axis_index_groups=groups)


def copies(block, n):
    return jnp.broadcast_to(block[None], (n, *block.shape))


def wide(tall_one):
    rows = tall_one.shape[0] // 2
    return jnp.concatenate([tall_one[:rows], tall_one[rows:]], axis=1)


def tall(wide_one):
    lanes = wide_one.shape[1] // 2
    return jnp.concatenate([wide_one[:, :lanes], wide_one[:, lanes:]], axis=0)


def three(value):
    out = []
    for _ in range(3):
        out.append(lax.reduce_precision(value, 8, 7))
        value = value - out[-1]
    return [v.astype(BF) for v in out]


def shards(out_grads, inputs, basis_out, basis_in, eig_out, eig_in, pair_order, length_bucket):
    tokens, share, block = pair_order.shape[0], inputs.shape[0], out_grads.shape[0]
    half = basis_in.shape[1]
    extra = 32 - share
    n = 16
    first = lax.axis_index("core") == 0
    zh, zl = lax.axis_index("zh"), lax.axis_index("zl")

    acts = jnp.concatenate([inputs, basis_out[:extra]], axis=0)
    grads = jnp.pad(out_grads, ((0, 64 - block), (0, 0)))
    grads = jnp.concatenate([grads[:32], grads[32:]], axis=1)
    kept = jnp.where(first, grads, acts)
    far = jnp.where(
        first, jnp.concatenate([acts, wide(basis_in)], axis=0), jnp.concatenate([grads, basis_out], axis=0)
    )
    far = lax.ppermute(far, "core", SWAP)
    far, basis_far = far[:32], far[32:]
    lanes = [[p[:, :half], p[:, half:]] for p in (kept, far)]
    as_grads = jnp.concatenate([jnp.concatenate(p, axis=0) for p in lanes], axis=1)
    as_acts = jnp.concatenate([far[:share], kept[:share], far[share:], kept[share:]], axis=0)
    rows = jnp.where(first, as_grads, as_acts)

    rows = both(rows, PAIR_IN)
    basis = jnp.where(
        first,
        jnp.concatenate([basis_out, basis_far], axis=0),
        jnp.concatenate([tall(basis_far), basis_in], axis=1),
    )

    parity = jnp.where(jnp.arange(tokens) % 2 == 0, 1.0, -1.0)
    token = lax.broadcasted_iota(jnp.int32, (1, tokens), 1)
    sign = jnp.sum(jnp.where(pair_order[:, None] == token, parity[:, None], 0.0), axis=0)
    weights = sign / jnp.sqrt((1.0 + length_bucket.astype(F32)) * tokens)
    weights = jnp.where(first, weights, 1.0)
    eig3 = jnp.concatenate([*three(eig_in), jnp.zeros((half,), BF)]).reshape(2, 2 * half)
    later = jnp.concatenate([wide(basis_in), jnp.pad(eig3, ((0, 14), (0, 0)))], axis=0)
    low = jnp.where(first, zh, zl // 2) == 0
    rows, basis, weights, later, low = lax.optimization_barrier((rows, basis, weights, later, low))
    rows = exchange(copies(rows, 8), EIGHT_IN)
    ordered = rows[:, :, :block].reshape(tokens, -1)
    paired = rows.reshape(4, 2, 2, 64, -1).swapaxes(1, 2)[:, :, :, :block].reshape(tokens, -1)
    part = dot(basis, jnp.where(first, paired, ordered), ((0,), (1,))).astype(BF)
    part = exchange(part.reshape(8, -1, tokens), EIGHT_MID)
    part, rows = lax.optimization_barrier((part, rows))
    total = jnp.sum(part.astype(F32), axis=0)

    totals = both(total.astype(BF), PAIR_MID)
    total_far = jnp.where(low, totals[1], totals[0])
    slab0, slab1 = (
        rows[:, :, block + k * extra : block + (k + 1) * extra].swapaxes(0, 1).reshape(n * extra, -1)
        for k in range(2)
    )
    packed = jnp.concatenate([slab0, later], axis=0)
    rot = ((total + total_far.astype(F32)) * weights).astype(BF)
    rot, packed, slab1 = lax.optimization_barrier((rot, packed, slab1))
    rot = exchange(copies(rot, 8), EIGHT_MID).reshape(-1, tokens)
    rot, packed = lax.optimization_barrier((rot, packed))
    rot_far = lax.ppermute(rot, "core", SWAP)
    far = lax.ppermute(packed, "core", SWAP)
    rot_far, far = lax.optimization_barrier((rot_far, far))
    slab = jnp.where(first, far[: slab1.shape[0]], slab1)
    eig_far = far[-16:-14].astype(F32).reshape(4, half)
    eig_far = eig_far[0] + eig_far[1] + eig_far[2]
    eig_in2 = jnp.where(first, jnp.concatenate([eig_in, eig_far]), jnp.concatenate([eig_far, eig_in]))
    in_far = tall(far[slab1.shape[0] : -16])
    basis_in2 = jnp.where(
        first, jnp.concatenate([basis_in, in_far], axis=1), jnp.concatenate([in_far, basis_in], axis=1)
    )

    middle = dot(rot, rot_far, ((1,), (1,)))
    down, across = jnp.where(first, eig_out, eig_in2), jnp.where(first, eig_in2, eig_out)
    scaled = (middle / (down[:, None] * across[None, :] + DAMPING)).astype(BF)
    left = jnp.where(first, dot(slab, scaled, ((1,), (0,))), dot(slab, scaled, ((1,), (1,))))

    left, basis_in2 = lax.optimization_barrier((left, basis_in2))
    left = lax.all_to_all(left.reshape(n, -1, left.shape[1]), ("x", "zl"), 0, 0, tiled=True)
    left = jnp.sum(left, axis=0).astype(BF)
    left = lax.all_to_all(copies(left, n), ("x", "zl"), 0, 0, tiled=True)
    left = left.reshape(-1, left.shape[2])
    final = dot(left, basis_in2, ((1,), (1,)))
    final = exchange(final.reshape(n, -1, final.shape[1]), COL_ALL[0] + COL_ALL[1])
    return jnp.sum(final, axis=0)


def solution(mesh):
    fine = Mesh(mesh.devices.reshape(SIZES), AXES)
    row, col = AXES[:2], AXES[2:]
    return jax.shard_map(
        shards,
        mesh=fine,
        in_specs=(P(row, col), P(col, row), P(col, row), P(row, col), P(row), P(col), P(), P()),
        out_specs=P(col, row),
        check_vma=False,
    )
```

```python
import jax
import jax.numpy as jnp
import numpy as np
from jax import lax
from jax.sharding import Mesh, PartitionSpec as P

DAMPING = 0.1
AXES = ("x", "zl", "y", "zh", "core")
SIZES = (4, 4, 8, 2, 2)
BF = jnp.bfloat16
F32 = jnp.float32
SWAP = [(0, 1), (1, 0)]

INDEX = np.arange(512).reshape(4, 2, 2, 8, 2, 2)


def lists(order, size):
    return INDEX.transpose(order).reshape(2, -1, size).tolist()


ROW_PAIR, ROW_EIGHT = lists((5, 0, 2, 3, 4, 1), 2), lists((5, 1, 3, 4, 0, 2), 8)
COL_PAIR, COL_EIGHT = lists((5, 0, 1, 2, 3, 4), 2), lists((5, 0, 1, 2, 4, 3), 8)
COL_ALL = lists((5, 0, 1, 2, 4, 3), 16)
EIGHT_IN = COL_EIGHT[0] + ROW_EIGHT[1]
EIGHT_MID = ROW_EIGHT[0] + [[g[3 * p % 8] for p in range(8)] for g in COL_EIGHT[1]]
PAIR_IN = COL_PAIR[0] + ROW_PAIR[1]
PAIR_MID = ROW_PAIR[0] + COL_PAIR[1]


def dot(a, b, contract):
    return lax.dot_general(a, b, (contract, ((), ())), preferred_element_type=F32)


def exchange(parts, groups):
    return lax.all_to_all(parts, AXES, 0, 0, axis_index_groups=groups, tiled=True)


def both(block, groups):
    return lax.all_gather(block, AXES, axis_index_groups=groups)


def copies(block, n):
    return jnp.broadcast_to(block[None], (n, *block.shape))


def wide(tall_one):
    rows = tall_one.shape[0] // 2
    return jnp.concatenate([tall_one[:rows], tall_one[rows:]], axis=1)


def tall(wide_one):
    lanes = wide_one.shape[1] // 2
    return jnp.concatenate([wide_one[:, :lanes], wide_one[:, lanes:]], axis=0)


def three(value):
    out = []
    for _ in range(3):
        out.append(lax.reduce_precision(value, 8, 7))
        value = value - out[-1]
    return [v.astype(BF) for v in out]


def shards(out_grads, inputs, basis_out, basis_in, eig_out, eig_in, pair_order, length_bucket):
    tokens, share, block = pair_order.shape[0], inputs.shape[0], out_grads.shape[0]
    half = basis_in.shape[1]
    extra = 32 - share
    n = 16
    first = lax.axis_index("core") == 0
    out_side = lax.axis_index("core") == 1
    zh, zl = lax.axis_index("zh"), lax.axis_index("zl")

    acts = jnp.concatenate([inputs, basis_out[:extra]], axis=0)
    grads = jnp.pad(out_grads, ((0, 64 - block), (0, 0)))
    grads = jnp.concatenate([grads[:32], grads[32:]], axis=1)
    kept = jnp.where(out_side, grads, acts)
    far = jnp.where(
        out_side, jnp.concatenate([acts, wide(basis_in)], axis=0), jnp.concatenate([grads, basis_out], axis=0)
    )
    far = lax.all_gather(far, "core")
    far = jnp.where(first, far[1], far[0])
    far, basis_far = far[:32], far[32:]
    lanes = [[p[:, :half], p[:, half:]] for p in (kept, far)]
    as_grads = jnp.concatenate([jnp.concatenate(p, axis=0) for p in lanes], axis=1)
    as_acts = jnp.concatenate([kept[:share], far[:share], kept[share:], far[share:]], axis=0)
    rows = jnp.where(out_side, as_grads, as_acts)

    rows = both(rows, PAIR_IN)
    basis = jnp.where(
        out_side,
        jnp.concatenate([basis_out, basis_far], axis=0),
        jnp.concatenate([basis_in, tall(basis_far)], axis=1),
    )

    parity = jnp.where(jnp.arange(tokens) % 2 == 0, 1.0, -1.0)
    token = lax.broadcasted_iota(jnp.int32, (1, tokens), 1)
    sign = jnp.sum(jnp.where(pair_order[:, None] == token, parity[:, None], 0.0), axis=0)
    weights = sign / jnp.sqrt((1.0 + length_bucket.astype(F32)) * tokens)
    weights = jnp.where(out_side, weights, 1.0)
    eig3 = jnp.concatenate([*three(eig_in), jnp.zeros((half,), BF)]).reshape(2, 2 * half)
    later = jnp.concatenate([wide(basis_in), jnp.pad(eig3, ((0, 14), (0, 0)))], axis=0)
    low = jnp.where(out_side, zh, zl // 2) == 0
    rows, basis, weights, later, low = lax.optimization_barrier((rows, basis, weights, later, low))
    rows = exchange(copies(rows, 8), EIGHT_IN)
    ordered = rows[:, :, :block].reshape(tokens, -1)
    paired = rows.reshape(4, 2, 2, 64, -1).swapaxes(1, 2)[:, :, :, :block].reshape(tokens, -1)
    part = dot(basis, jnp.where(out_side, paired, ordered), ((0,), (1,))).astype(BF)
    part = exchange(part.reshape(8, -1, tokens), EIGHT_MID)
    part, rows = lax.optimization_barrier((part, rows))
    total = jnp.sum(part.astype(F32), axis=0)

    totals = both(total.astype(BF), PAIR_MID)
    total_far = jnp.where(low, totals[1], totals[0])
    slab0, slab1 = (
        rows[:, :, block + k * extra : block + (k + 1) * extra].swapaxes(0, 1).reshape(n * extra, -1)
        for k in range(2)
    )
    packed = jnp.concatenate([slab1, later], axis=0)
    rot = ((total + total_far.astype(F32)) * weights).astype(BF)
    rot, packed, slab0 = lax.optimization_barrier((rot, packed, slab0))
    rot = exchange(copies(rot, 8), EIGHT_MID).reshape(-1, tokens)
    rot, packed = lax.optimization_barrier((rot, packed))
    rot_far = lax.ppermute(rot, "core", SWAP)
    far = lax.ppermute(packed, "core", SWAP)
    rot_far, far = lax.optimization_barrier((rot_far, far))
    slab = jnp.where(out_side, far[: slab0.shape[0]], slab0)
    eig_far = far[-16:-14].astype(F32).reshape(4, half)
    eig_far = eig_far[0] + eig_far[1] + eig_far[2]
    eig_in2 = jnp.where(first, jnp.concatenate([eig_in, eig_far]), jnp.concatenate([eig_far, eig_in]))
    in_far = tall(far[slab0.shape[0] : -16])
    basis_in2 = jnp.where(
        first, jnp.concatenate([basis_in, in_far], axis=1), jnp.concatenate([in_far, basis_in], axis=1)
    )

    middle = dot(rot, rot_far, ((1,), (1,)))
    down, across = jnp.where(out_side, eig_out, eig_in2), jnp.where(out_side, eig_in2, eig_out)
    scaled = (middle / (down[:, None] * across[None, :] + DAMPING)).astype(BF)
    left = jnp.where(out_side, dot(slab, scaled, ((1,), (0,))), dot(slab, scaled, ((1,), (1,))))

    left, basis_in2 = lax.optimization_barrier((left, basis_in2))
    left = exchange(left.reshape(8, -1, left.shape[1]), ROW_EIGHT[0] + ROW_EIGHT[1])
    left = both(jnp.sum(left, axis=0), ROW_PAIR[0] + ROW_PAIR[1])
    left = exchange(copies((left[0] + left[1]).astype(BF), 8), ROW_EIGHT[0] + ROW_EIGHT[1])
    left = left.reshape(-1, left.shape[2])
    final = dot(left, basis_in2, ((1,), (1,)))
    final = exchange(final.reshape(n, -1, final.shape[1]), COL_ALL[0] + COL_ALL[1])
    return jnp.sum(final, axis=0)


def solution(mesh):
    fine = Mesh(mesh.devices.reshape(SIZES), AXES)
    row, col = AXES[:2], AXES[2:]
    return jax.shard_map(
        shards,
        mesh=fine,
        in_specs=(P(row, col), P(col, row), P(col, row), P(row, col), P(row), P(col), P(), P()),
        out_specs=P(col, row),
        check_vma=False,
    )
```

```python
import jax
import jax.numpy as jnp
import numpy as np
from jax import lax
from jax.sharding import Mesh, PartitionSpec as P

DAMPING = 0.1
AXES = ("x", "zl", "y", "zh", "core")
SIZES = (4, 4, 8, 2, 2)
BF = jnp.bfloat16
F32 = jnp.float32
SWAP = [(0, 1), (1, 0)]

INDEX = np.arange(512).reshape(4, 2, 2, 8, 2, 2)


def lists(order, size):
    return INDEX.transpose(order).reshape(2, -1, size).tolist()


ROW_PAIR, ROW_EIGHT = lists((5, 0, 2, 3, 4, 1), 2), lists((5, 1, 3, 4, 0, 2), 8)
NEAR_PAIR, NEAR_EIGHT = lists((5, 0, 1, 3, 4, 2), 2), lists((5, 2, 3, 4, 0, 1), 8)
COL_PAIR, COL_EIGHT = lists((5, 0, 1, 2, 3, 4), 2), lists((5, 0, 1, 2, 4, 3), 8)
COL_ALL = lists((5, 0, 1, 2, 4, 3), 16)
EIGHT_IN = COL_EIGHT[0] + ROW_EIGHT[1]
EIGHT_MID = ROW_EIGHT[0] + [[g[3 * p % 8] for p in range(8)] for g in COL_EIGHT[1]]
PAIR_IN = COL_PAIR[0] + ROW_PAIR[1]
PAIR_MID = ROW_PAIR[0] + COL_PAIR[1]


def dot(a, b, contract):
    return lax.dot_general(a, b, (contract, ((), ())), preferred_element_type=F32)


def exchange(parts, groups):
    return lax.all_to_all(parts, AXES, 0, 0, axis_index_groups=groups, tiled=True)


def both(block, groups):
    return lax.all_gather(block, AXES, axis_index_groups=groups)


def copies(block, n):
    return jnp.broadcast_to(block[None], (n, *block.shape))


def wide(tall_one):
    rows = tall_one.shape[0] // 2
    return jnp.concatenate([tall_one[:rows], tall_one[rows:]], axis=1)


def tall(wide_one):
    lanes = wide_one.shape[1] // 2
    return jnp.concatenate([wide_one[:, :lanes], wide_one[:, lanes:]], axis=0)


def three(value):
    out = []
    for _ in range(3):
        out.append(lax.reduce_precision(value, 8, 7))
        value = value - out[-1]
    return [v.astype(BF) for v in out]


def shards(out_grads, inputs, basis_out, basis_in, eig_out, eig_in, pair_order, length_bucket):
    tokens, share, block = pair_order.shape[0], inputs.shape[0], out_grads.shape[0]
    half = basis_in.shape[1]
    extra = 32 - share
    n = 16
    first = lax.axis_index("core") == 0
    out_side = lax.axis_index("core") == 1
    zh, zl = lax.axis_index("zh"), lax.axis_index("zl")

    acts = jnp.concatenate([inputs, basis_out[:extra]], axis=0)
    grads = jnp.pad(out_grads, ((0, 64 - block), (0, 0)))
    grads = jnp.concatenate([grads[:32], grads[32:]], axis=1)
    kept = jnp.where(out_side, grads, acts)
    far = jnp.where(
        out_side, jnp.concatenate([acts, wide(basis_in)], axis=0), jnp.concatenate([grads, basis_out], axis=0)
    )
    far = lax.all_gather(far, "core")
    far = jnp.where(first, far[1], far[0])
    far, basis_far = far[:32], far[32:]
    lanes = [[p[:, :half], p[:, half:]] for p in (kept, far)]
    as_grads = jnp.concatenate([jnp.concatenate(p, axis=0) for p in lanes], axis=1)
    as_acts = jnp.concatenate([kept[:share], far[:share], kept[share:], far[share:]], axis=0)
    rows = jnp.where(out_side, as_grads, as_acts)

    rows = both(rows, PAIR_IN)
    basis = jnp.where(
        out_side,
        jnp.concatenate([basis_out, basis_far], axis=0),
        jnp.concatenate([basis_in, tall(basis_far)], axis=1),
    )

    parity = jnp.where(jnp.arange(tokens) % 2 == 0, 1.0, -1.0)
    token = lax.broadcasted_iota(jnp.int32, (1, tokens), 1)
    sign = jnp.sum(jnp.where(pair_order[:, None] == token, parity[:, None], 0.0), axis=0)
    weights = sign / jnp.sqrt((1.0 + length_bucket.astype(F32)) * tokens)
    weights = jnp.where(out_side, weights, 1.0)
    eig3 = jnp.concatenate([*three(eig_in), jnp.zeros((half,), BF)]).reshape(2, 2 * half)
    later = jnp.concatenate([wide(basis_in), jnp.pad(eig3, ((0, 14), (0, 0)))], axis=0)
    low = jnp.where(out_side, zh, zl // 2) == 0
    rows, basis, weights, later, low = lax.optimization_barrier((rows, basis, weights, later, low))
    rows = exchange(copies(rows, 8), EIGHT_IN)
    ordered = rows[:, :, :block].reshape(tokens, -1)
    paired = rows.reshape(4, 2, 2, 64, -1).swapaxes(1, 2)[:, :, :, :block].reshape(tokens, -1)
    part = dot(basis, jnp.where(out_side, paired, ordered), ((0,), (1,))).astype(BF)
    part = exchange(part.reshape(8, -1, tokens), EIGHT_MID)
    part, rows = lax.optimization_barrier((part, rows))
    total = jnp.sum(part.astype(F32), axis=0)

    totals = both(total.astype(BF), PAIR_MID)
    total_far = jnp.where(low, totals[1], totals[0])
    slab0, slab1 = (
        rows[:, :, block + k * extra : block + (k + 1) * extra].swapaxes(0, 1).reshape(n * extra, -1)
        for k in range(2)
    )
    packed = jnp.concatenate([slab1, later], axis=0)
    rot = ((total + total_far.astype(F32)) * weights).astype(BF)
    rot, packed, slab0 = lax.optimization_barrier((rot, packed, slab0))
    rot = exchange(copies(rot, 8), EIGHT_MID).reshape(-1, tokens)
    rot, packed = lax.optimization_barrier((rot, packed))
    rot_far = lax.ppermute(rot, "core", SWAP)
    far = lax.ppermute(packed, "core", SWAP)
    rot_far, far = lax.optimization_barrier((rot_far, far))
    slab = jnp.where(out_side, far[: slab0.shape[0]], slab0)
    eig_far = far[-16:-14].astype(F32).reshape(4, half)
    eig_far = eig_far[0] + eig_far[1] + eig_far[2]
    eig_in2 = jnp.where(first, jnp.concatenate([eig_in, eig_far]), jnp.concatenate([eig_far, eig_in]))
    in_far = tall(far[slab0.shape[0] : -16])
    basis_in2 = jnp.where(
        first, jnp.concatenate([basis_in, in_far], axis=1), jnp.concatenate([in_far, basis_in], axis=1)
    )

    middle = dot(rot, rot_far, ((1,), (1,)))
    down, across = jnp.where(out_side, eig_out, eig_in2), jnp.where(out_side, eig_in2, eig_out)
    scaled = (middle / (down[:, None] * across[None, :] + DAMPING)).astype(BF)
    left = jnp.where(out_side, dot(slab, scaled, ((1,), (0,))), dot(slab, scaled, ((1,), (1,))))

    left, basis_in2 = lax.optimization_barrier((left, basis_in2))
    left = exchange(left.reshape(8, -1, left.shape[1]), NEAR_EIGHT[0] + NEAR_EIGHT[1])
    left = both(jnp.sum(left, axis=0), NEAR_PAIR[0] + NEAR_PAIR[1])
    left = exchange(copies((left[0] + left[1]).astype(BF), 8), NEAR_EIGHT[0] + NEAR_EIGHT[1])
    left = left.reshape(-1, left.shape[2])
    final = dot(left, basis_in2, ((1,), (1,)))
    final = exchange(final.reshape(n, -1, final.shape[1]), COL_ALL[0] + COL_ALL[1])
    return jnp.sum(final, axis=0)


def solution(mesh):
    fine = Mesh(mesh.devices.reshape(SIZES), AXES)
    row, col = AXES[:2], AXES[2:]
    return jax.shard_map(
        shards,
        mesh=fine,
        in_specs=(P(row, col), P(col, row), P(col, row), P(row, col), P(row), P(col), P(), P()),
        out_specs=P(col, row),
        check_vma=False,
    )
```
